256 devices in a mesh: layer: 8 (over y, z_hi), latent: 32 (over z_lo, x, core).
Axes of the slice: x: 4, y: 4, z: 8 (z_hi: 2, z_lo: 4; z = z_hi * 4 + z_lo), core: 2. Of those that a mesh axis runs over, the one named last changes fastest.
Arguments:
- acts: bfloat16 [512, 8, 2048], P(None, 'layer'), may hold values from -6 to 6
- mask: int32 [512, 16384], P(None, 'latent'), may hold values 0 or 1
- w_enc: bfloat16 [8, 2048, 16384], P('layer', None, 'latent'), may hold values from -0.046875 to 0.046875
- b_enc: float32 [16384], P('latent'), may hold values from -3 to 3
- w_dec: bfloat16 [16384, 8, 2048], P('latent', 'layer'), may hold values from -8 to 8
- b_dec: float32 [8, 2048], P('layer'), may hold values from -3 to 3
Outputs:
- grad_enc: bfloat16 [8, 2048, 16384], P('layer', None, 'latent')
- grad_dec: bfloat16 [16384, 8, 2048], P('latent', 'layer')
The draws below stay inside these ranges and needn't reach their ends.
All inputs are finite; a program needn't handle non-finite values. No bound on the sum of `mask` on one device may be relied on, other than what follows from the above.
Results may differ from the reference program's by a relative error of at most 0.007.
Values may be sent and summed in bfloat16 or wider, within the bound.
No kernel may reach another device: no remote copies, remote signals or barrier semaphores. Data moves between devices by JAX's collectives and lax.ppermute only.
A program may use at most 64 MiB of HBM per device.

```python
import math
import jax
import jax.numpy as jnp
from jax import lax

D = 2048
B = 512
F = 16384
L = 8


def draw_w_dec(key, part):
    key = jax.random.fold_in(key, 7)
    first, second = jax.random.split(key, 2)
    base = jnp.clip(jax.random.normal(first, (F, L, D), jnp.float32), -4.0, 4.0)
    layer_scale = 3.0 ** (jnp.arange(L, dtype=jnp.float32) / max(L - 1, 1))
    latent_scale = jnp.exp(jax.random.uniform(second, (F,), jnp.float32, 0.0, math.log(10.0)))
    values = base * 0.5 * F ** (-0.5) * latent_scale[:, None, None] * layer_scale[None, :, None]
    return values.astype(jnp.bfloat16)


def with_ends(entries, rng, least, largest):
    longest = entries.shape.index(max(entries.shape))
    spots = []
    for shift in (0, 1):
        where = [jax.random.randint(jax.random.fold_in(rng, axis), (), 0, length) for axis, length in enumerate(entries.shape)]
        where[longest] = (where[longest] + shift) % entries.shape[longest]
        spots.append(tuple(where))
    return entries.at[spots[0]].set(least).at[spots[1]].set(largest)


def level_of(key, shape, cuts, smallest, top_value):
    def one(position, blocks):
        steps = jax.random.uniform(jax.random.fold_in(jax.random.fold_in(key, 6), position), (blocks,), jnp.float32, smallest / len(cuts), top_value / len(cuts))
        return jnp.repeat(jnp.exp(steps), shape[position] // blocks).reshape((-1,) + (1,) * (len(shape) - position - 1))

    factor_of = one(*cuts[0])
    for cut in cuts[1:]:
        factor_of = factor_of * one(*cut)
    return factor_of


def scatter_about(rng, extent, scale, most, cuts=(), held_as=jnp.bfloat16):
    array = scale * jax.random.normal(rng, extent, jnp.float32)
    if cuts:
        array = array * level_of(rng, extent, cuts, -0.22, 0.18)
    return jnp.clip(array, -most, most).astype(held_as)


def setup_inputs(seed: int = 0) -> dict:
    key_of = jax.random.split(jax.random.key(seed), 7)
    acts = scatter_about(key_of[0], (B, L, D), 1.0, 6.0, ((1, 8),))
    mask = with_ends((jax.random.randint(key_of[1], (B, F), 0, 3) < 1).astype(jnp.int32), jax.random.fold_in(key_of[1], 1), 0, 1)
    w_enc = scatter_about(key_of[2], (L, D, F), (L * D) ** -0.5, 0.046875, ((0, 8), (2, 32)))
    b_enc = scatter_about(key_of[3], (F,), 0.5, 3.0, ((0, 32),), jnp.float32)
    w_dec = draw_w_dec(jax.random.fold_in(key_of[6], 71), 0)
    b_dec = scatter_about(key_of[5], (L, D), 0.5, 3.0, ((0, 8),), jnp.float32)
    return {"acts": acts, "mask": mask, "w_enc": w_enc, "b_enc": b_enc, "w_dec": w_dec, "b_dec": b_dec}


loss_scale = 0.0625
sparsity = 0.25

def reference(acts, mask, w_enc, b_enc, w_dec, b_dec):
    rows = acts.shape[0]
    flat = acts.reshape(rows, L * D)
    pre = jnp.dot(flat, w_enc.reshape(L * D, F), preferred_element_type=jnp.float32) + b_enc.astype(jnp.float32)
    active = mask.astype(jnp.float32)
    codes = (active * pre).astype(jnp.bfloat16)
    wide = w_dec.astype(jnp.float32)
    lengths = jnp.sqrt(lax.optimization_barrier(jnp.sum(wide * wide, axis=2)) + 1e-06)
    norms = lax.optimization_barrier(jnp.sum(lengths, axis=1))
    dec_flat = w_dec.reshape(F, L * D)
    recon = jnp.dot(codes, dec_flat, preferred_element_type=jnp.float32) + b_dec.reshape(L * D).astype(jnp.float32)
    error = (recon - flat.astype(jnp.float32)).astype(jnp.bfloat16)
    back = lax.dot_general(error, dec_flat, (((1,), (1,)), ((), ())), preferred_element_type=jnp.float32)
    dpre = (loss_scale * active * (back + sparsity * norms[None, :])).astype(jnp.bfloat16)
    grad_enc = lax.dot_general(flat, dpre, (((0,), (0,)), ((), ())), preferred_element_type=jnp.float32)
    grad_enc = grad_enc.reshape(L, D, F).astype(jnp.bfloat16)
    usage = lax.optimization_barrier(jnp.sum(codes.astype(jnp.float32), axis=0))
    cross = lax.dot_general(codes, error, (((0,), (0,)), ((), ())), preferred_element_type=jnp.float32)
    grad_dec = loss_scale * (cross.reshape(F, L, D) + sparsity * usage[:, None, None] * wide / lengths[:, :, None])
    return (grad_enc, grad_dec.astype(jnp.bfloat16))
```

```python
import jax
import jax.numpy as jnp
from jax import lax
from jax.sharding import PartitionSpec as P

loss_scale = 0.0625
sparsity = 0.25
bf16 = jnp.bfloat16
f32 = jnp.float32


def layer_perm(dy, flip):
    return [(i, (((i // 2) + dy) % 4) * 2 + ((i % 2) ^ flip)) for i in range(8)]


def latent_perm(dx=0, zxor=0, cxor=0):
    out = []
    for i in range(32):
        z, x, c = i // 8, (i // 2) % 4, i % 2
        out.append((i, ((z ^ zxor) * 4 + (x + dx) % 4) * 2 + (c ^ cxor)))
    return out


def shift_y(v, k):
    return lax.ppermute(v, "layer", layer_perm(k, 0))


def swap_h(v):
    return lax.ppermute(v, "layer", layer_perm(0, 1))


def shift_x(v, k):
    return lax.ppermute(v, "latent", latent_perm(dx=k))


def xor_z(v, k):
    return lax.ppermute(v, "latent", latent_perm(zxor=k))


def swap_c(v):
    return lax.ppermute(v, "latent", latent_perm(cxor=1))


def block(v, index, size, axis):
    return lax.dynamic_slice_in_dim(v, index * size, size, axis)


def roll_blocks(v, shift, axis):
    return lax.dynamic_slice_in_dim(
        jnp.concatenate([v, v], axis), shift, v.shape[axis], axis
    )


def dot(a, b):
    return jnp.dot(a, b, preferred_element_type=f32)


def dot_t(a, b):
    return lax.dot_general(a, b, (((1,), (1,)), ((), ())), preferred_element_type=f32)


def body(acts, mask, w_enc, b_enc, w_dec, b_dec):
    rows, _, width = acts.shape
    latents = w_enc.shape[2]
    ny, nx, nz = 4, 4, 4
    rb = rows // ny
    r = rb // nx
    half = width // 2
    q = half // nz
    y = lax.axis_index("layer") // 2
    la = lax.axis_index("latent")
    z, x, c = la // 8, (la // 2) % 4, la % 2

    flat = acts.reshape(rows, width)
    enc = w_enc.reshape(width, latents)
    dec = w_dec.reshape(latents, width)

    dec_own = block(dec, c, half, 1)
    dec_other = swap_c(block(dec, 1 - c, half, 1))

    partial = dot(flat, enc)
    got = [shift_y(block(partial, (y + k) % ny, rb, 0).astype(bf16), k) for k in (2, 1, 3)]
    mine = block(partial, y, rb, 0)
    for g in got:
        mine = mine + g.astype(f32)
    pre = mine + swap_h(mine.astype(bf16)).astype(f32) + b_enc[None, :]
    active = block(mask, y, rb, 0).astype(f32)
    shard = (active * pre).astype(bf16)
    shard = roll_blocks(shard.reshape(nx, r, latents), x, 0)
    codes = [shard] + [shift_y(shard, -k) for k in (1, 2, 3)]
    codes = jnp.stack(codes)
    codes_other = swap_c(codes)

    def piece(k):
        return dot(codes[:, k].reshape(rb, latents), dec_own) + dot(
            codes_other[:, k].reshape(rb, latents), dec_other
        )

    got = [shift_x(piece(k).astype(bf16), k) for k in (2, 1, 3)]
    total = piece(0)
    for g in got:
        total = total + g.astype(f32)
    got = [xor_z(block(total, z ^ k, q, 1).astype(bf16), k) for k in (3, 2, 1)]
    recon = block(total, z, q, 1)
    for g in got:
        recon = recon + g.astype(f32)
    column = c * half + z * q
    acts_here = lax.dynamic_slice(flat.reshape(ny, nx, r, width), (0, x, 0, column), (ny, 1, r, q))
    acts_here = roll_blocks(acts_here, y, 0).reshape(rb, q).astype(f32)
    bias_here = lax.dynamic_slice(b_dec, (0, column), (1, q))
    error = (recon + bias_here - acts_here).astype(bf16)
    parts = [error] + [xor_z(error, k) for k in (1, 2, 3)]
    spread = []
    for m in range(nz):
        v = parts[0]
        for k in (1, 2, 3):
            v = jnp.where((z ^ k) == m, parts[k], v)
        spread.append(v)
    error = jnp.concatenate(spread, axis=1)
    errors = [error] + [shift_x(error, -k) for k in (1, 2, 3)]
    others = [swap_c(e) for e in errors]
    first = c == 0
    errors = [
        jnp.concatenate([jnp.where(first, e, o), jnp.where(first, o, e)], axis=1)
        for e, o in zip(errors, others)
    ]

    wide = dec.astype(f32)
    lengths = jnp.sqrt(jnp.sum(wide * wide, axis=1) + 1e-06)
    back = jnp.stack([dot_t(e, dec).reshape(ny, r, latents) for e in errors], axis=1)
    back = back + sparsity * lengths
    got = [shift_y(back[k].astype(bf16), k) for k in (2, 1, 3)]
    mine = back[0]
    for g in got:
        mine = mine + g.astype(f32)
    mine = mine + swap_h(mine.astype(bf16)).astype(f32)
    active_rolled = roll_blocks(active.reshape(nx, r, latents), x, 0)
    shard = (loss_scale * active_rolled * mine).astype(bf16)
    dpre = jnp.concatenate([shard] + [shift_y(shard, -k) for k in (1, 2, 3)])
    dpre = dpre.reshape(rows, latents)

    acts_rolled = flat.reshape(ny, nx, r, width)
    acts_rolled = roll_blocks(roll_blocks(acts_rolled, y, 0), x, 1).reshape(rows, width)
    grad_enc = lax.dot_general(
        acts_rolled, dpre, (((0,), (0,)), ((), ())), preferred_element_type=f32
    )
    grad_enc = grad_enc.astype(bf16).reshape(w_enc.shape)

    usage = jnp.sum(codes.astype(f32), axis=(0, 1, 2))
    codes_x = codes.swapaxes(0, 1).reshape(rows, latents)
    cross = lax.dot_general(
        codes_x, jnp.concatenate(errors), (((0,), (0,)), ((), ())), preferred_element_type=f32
    )
    grad_dec = loss_scale * (cross + (sparsity * usage / lengths)[:, None] * wide)
    return (grad_enc, grad_dec.astype(bf16).reshape(w_dec.shape))


def solution(mesh):
    return jax.shard_map(
        body,
        mesh=mesh,
        in_specs=(
            P(None, "layer", None),
            P(None, "latent"),
            P("layer", None, "latent"),
            P("latent"),
            P("latent", "layer", None),
            P("layer", None),
        ),
        out_specs=(P("layer", None, "latent"), P("latent", "layer", None)),
        check_vma=False,
    )
```

```python
import jax
import jax.numpy as jnp
from jax import lax
from jax.experimental import pallas as pl
from jax.experimental.pallas import tpu as pltpu
from jax.sharding import PartitionSpec as P

loss_scale = 0.0625
sparsity = 0.25
bf16 = jnp.bfloat16
f32 = jnp.float32
MIB = 1024 * 1024
LIMIT = pltpu.CompilerParams(vmem_limit_bytes=40 * MIB)
FIRST = pltpu.CompilerParams(vmem_limit_bytes=56 * MIB)
after = lax.optimization_barrier


def place():
    y = lax.axis_index("layer") // 2
    latent = lax.axis_index("latent")
    return y, latent // 2 % 4, latent // 8, latent % 2


def ahead(v, k):
    return (v + k) % 4


def exchange(v, axis, k=1):
    perm = []
    for i in range(256):
        layer, latent = i // 32, i % 32
        y, h = layer // 2, layer % 2
        z, x, c = latent // 8, (latent // 2) % 4, latent % 2
        if axis == "y":
            y = ahead(y, k)
        elif axis == "x":
            x = ahead(x, k)
        elif axis == "z":
            z ^= k
        elif axis == "h":
            h ^= k
        else:
            c ^= k
        perm.append((i, (y * 2 + h) * 32 + (z * 4 + x) * 2 + c))
    return lax.ppermute(v, ("layer", "latent"), perm)


FAR_FIRST = (2, 1, 3)
PARTS = 4
LINE = (3, 2, 1)


def gather(v, axis, ks):
    got = {k: exchange(v, axis, k if axis == "z" else -k) for k in ks}
    return [v, got[1], got[2], got[3]]


def sds(shape, dtype):
    return jax.ShapeDtypeStruct(shape, dtype)


def cost(flops, size):
    return pl.CostEstimate(flops=flops, bytes_accessed=size, transcendentals=0)


def local(kernel, outs, *args, flops=0, scratch=()):
    in_specs = [
        pl.BlockSpec(memory_space=pltpu.SMEM if a.dtype == jnp.int32 and a.ndim == 1 else pltpu.VMEM) for a in args
    ]
    size = sum(a.size * a.dtype.itemsize for a in args) + sum(o.size * o.dtype.itemsize for o in outs)
    return pl.pallas_call(
        kernel,
        out_shape=outs,
        in_specs=in_specs,
        out_specs=[pl.BlockSpec(memory_space=pltpu.VMEM) for _ in outs],
        scratch_shapes=scratch,
        compiler_params=LIMIT,
        cost_estimate=cost(flops, size),
    )(*args)


def dot(a, b):
    return jnp.dot(a, b, preferred_element_type=f32)


def dot_t(a, b):
    return lax.dot_general(a, b, (((1,), (1,)), ((), ())), preferred_element_type=f32)


def wide(ref):
    return ref[...].astype(f32)


def pre_kernel(acts, enc, *refs):
    sends, keep, total, acts_here, enc_here, sems = refs[:3], *refs[3:]
    m = keep.shape[0]
    k = acts.shape[1] // PARTS
    copies = []
    for i in range(PARTS):
        part = slice(i * k, (i + 1) * k)
        pair = (
            pltpu.make_async_copy(acts.at[:, part], acts_here.at[:, part], sems.at[0, i]),
            pltpu.make_async_copy(enc.at[part, :], enc_here.at[part, :], sems.at[1, i]),
        )
        for copy in pair:
            copy.start()
        copies.append(pair)
    for i, pair in enumerate(copies):
        part = slice(i * k, (i + 1) * k)
        for copy in pair:
            copy.wait()
        value = dot(acts_here[:, part], enc_here[part, :])
        total[...] = value if i == 0 else total[...] + value
    y = place()[0]
    for j, ref in enumerate((keep, *sends)):
        ref[...] = total[pl.ds(pl.multiple_of(ahead(y, j) * m, m), m), :].astype(ref.dtype)


def sum_kernel(keep, a, b, c, out, send):
    total = keep[...] + wide(a) + wide(b) + wide(c)
    out[...] = total
    send[...] = total.astype(bf16)


def codes_kernel(keep, got, bias, active, out):
    r = keep.shape[0] // 4
    for j in range(4):
        rows = pl.ds(pl.multiple_of(ahead(place()[1], j) * r, r), r)
        pre = keep[rows, :] + got[rows, :].astype(f32) + bias[...]
        out[j * r : (j + 1) * r, :] = (active[j * r : (j + 1) * r, :] * pre).astype(bf16)


def recon_own_kernel(*refs):
    own, dec, out, lhs = refs[:4], *refs[4:]
    ny = own[0].shape[0]
    r, half = ny // 4, dec.shape[1] // 2
    for b in range(4):
        for a in range(4):
            lhs[b * ny + a * r : b * ny + (a + 1) * r, :] = own[a][b * r : (b + 1) * r, :]
    c = place()[3]
    out[...] = dot(lhs[...], dec[:, pl.ds(pl.multiple_of(c * half, half), half)])


def recon_kernel(blocks, *refs):
    other, dec, own, outs, lhs = refs[:4], refs[4], refs[5], refs[6:-1], refs[-1]
    ny = other[0].shape[0]
    r = ny // 4
    for i, b in enumerate(blocks):
        for a in range(4):
            lhs[i * ny + a * r : i * ny + (a + 1) * r, :] = other[a][b * r : (b + 1) * r, :]
    value = dot(lhs[...], dec[...])
    for i, (b, out) in enumerate(zip(blocks, outs)):
        out[...] = (value[i * ny : (i + 1) * ny] + own[b * ny : (b + 1) * ny, :]).astype(out.dtype)


def split_kernel(keep, a, b, c, out, *sends):
    q = out.shape[1]
    for j, ref in enumerate((out, *sends)):
        column = pl.ds(pl.multiple_of((place()[2] ^ j) * q, q), q)
        total = keep[:, column] + a[:, column].astype(f32) + b[:, column].astype(f32) + c[:, column].astype(f32)
        ref[...] = total.astype(ref.dtype)


def error_kernel(keep, a, b, c, offset, out):
    out[...] = (keep[...] + wide(a) + wide(b) + wide(c) + offset[...]).astype(bf16)


def columns_kernel(a, b, c, d, out):
    q = a.shape[1]
    for j, ref in enumerate((a, b, c, d)):
        out[:, pl.ds(pl.multiple_of((place()[2] ^ j) * q, q), q)] = ref[...]


def back_own_kernel(*refs):
    own, dec, extra, error, out = refs[:4], *refs[4:]
    rows, half = error.shape
    r, ny = rows // 16, rows // 4
    for a in range(4):
        for b in range(4):
            error[a * ny + b * r : a * ny + (b + 1) * r, :] = own[b][a * r : (a + 1) * r, :]
    c = place()[3]
    out[...] = dot_t(error[...], dec[:, pl.ds(pl.multiple_of(c * half, half), half)]) + sparsity * extra[...]


def back_kernel(*refs):
    other, dec, own, error = refs[:4], *refs[4:7]
    sends, keep = refs[7:10], refs[10]
    rows, half = error.shape
    r, ny = rows // 16, rows // 4
    for a in range(4):
        for b in range(4):
            error[a * ny + b * r : a * ny + (b + 1) * r, :] = other[b][a * r : (a + 1) * r, :]
    c = 1 - place()[3]
    total = own[...] + dot_t(error[...], dec[:, pl.ds(pl.multiple_of(c * half, half), half)])
    for j, ref in enumerate((keep, *sends)):
        ref[...] = total[j * ny : (j + 1) * ny].astype(ref.dtype)


def dpre_kernel(keep, got, active, out):
    out[...] = (loss_scale * active[...] * (keep[...] + wide(got))).astype(bf16)


def copy_kernel(idx, src, out):
    out[...] = src[...].astype(out.dtype)


def offset_kernel(idx, acts, bias, out):
    out[...] = bias[...] - wide(acts)


def turn_acts_kernel(idx, a, b, c, d, out):
    out[...] = jnp.concatenate([a[...], b[...], c[...], d[...]], 0).T


def turn_codes_kernel(a, b, c, d, lengths, out, factor):
    m = a.shape[0]
    for j, ref in enumerate((a, b, c, d)):
        out[:, j * m : (j + 1) * m] = ref[...].T
    usage = jnp.sum(wide(out), axis=1, keepdims=True)
    factor[...] = sparsity * usage / lengths[...]


def cross_kernel(codes, own, other, dec, factor, out):
    half = own.shape[1]
    for c, ref in ((place()[3], own), (1 - place()[3], other)):
        at = pl.ds(pl.multiple_of(c * half, half), half)
        out[:, at] = (loss_scale * (dot(codes[...], ref[...]) + factor[...] * dec[:, at].astype(f32))).astype(bf16)


def grad_kernel(acts, a, b, c, d, out, rhs):
    m, n = a.shape[0], out.shape[0]
    step = pl.program_id(0)

    @pl.when(step == 0)
    def _():
        for j, ref in enumerate((a, b, c, d)):
            rhs[j * m : (j + 1) * m, :] = ref[...]

    out[...] = dot(acts[pl.ds(pl.multiple_of(step * n, n), n), :], rhs[...]).astype(bf16)


def placed(kernel, idx, grid, ins, outs, *args, flops=0, size=MIB, scratch=(), limit=LIMIT):
    return pl.pallas_call(
        kernel,
        out_shape=[sds(o[0], o[1]) for o in outs],
        grid_spec=pltpu.PrefetchScalarGridSpec(
            num_scalar_prefetch=1,
            grid=(grid,),
            in_specs=[pl.BlockSpec(*i) for i in ins],
            out_specs=[pl.BlockSpec(*o[2:]) for o in outs],
            scratch_shapes=scratch,
        ),
        compiler_params=limit,
        cost_estimate=cost(flops, size),
    )(idx, *args)


def body(acts, mask, w_enc, b_enc, w_dec, b_dec):
    rows, _, width = acts.shape
    latents = w_enc.shape[2]
    ny = rows // 4
    r = ny // 4
    half = width // 2
    q = half // 4
    y, x, z, c = place()
    blocks = [ahead(v, k) for v in (y, x) for k in range(4)] + [z ^ k for k in range(4)]
    idx = jnp.stack(blocks + [c, 1 - c]).astype(jnp.int32)
    matmul = 2 * rows * width * latents

    flat = acts.reshape(rows, width)
    enc = w_enc.reshape(width, latents)
    dec = w_dec.reshape(latents, width)
    tile = sds((ny, latents), bf16)

    whole = lambda j, idx: (0, 0)
    *sends, keep = pl.pallas_call(
        pre_kernel,
        out_shape=[tile] * 3 + [sds((ny, latents), f32)],
        in_specs=[pl.BlockSpec(memory_space=pl.ANY)] * 2,
        out_specs=[pl.BlockSpec(memory_space=pltpu.VMEM)] * 4,
        scratch_shapes=[
            pltpu.VMEM((rows, latents), f32),
            pltpu.VMEM((rows, width), bf16),
            pltpu.VMEM((width, latents), bf16),
            pltpu.SemaphoreType.DMA((2, PARTS)),
        ],
        compiler_params=FIRST,
        cost_estimate=cost(matmul, 6 * MIB),
    )(flat, enc)

    def over_layers(sends, keep):
        got = {j: exchange(sends[j - 1], "y", j) for j in FAR_FIRST}
        keep, send = local(sum_kernel, [sds((ny, latents), f32), tile], keep, got[1], got[2], got[3])
        return keep, exchange(send, "h")

    keep, got = over_layers(sends, keep)

    dec_a, mask_a, flat_a, _ = after((dec, mask, flat, keep))
    (dec_send,) = placed(
        copy_kernel, idx, 1, [((latents, half), lambda j, idx: (0, idx[13]))],
        [((latents, half), bf16, (latents, half), whole)], dec_a, size=2 * MIB,
    )
    dec_other = exchange(dec_send, "c")
    (active,) = placed(
        copy_kernel, idx, 4, [((r, latents), lambda j, idx: (idx[0] * 4 + idx[4 + j], 0))],
        [((ny, latents), f32, (r, latents), lambda j, idx: (j, 0))], mask_a,
    )
    (offset,) = placed(
        offset_kernel, idx, 4,
        [
            ((r, q), lambda j, idx: (idx[j] * 4 + idx[4], idx[12] * 4 + idx[8])),
            ((1, q), lambda j, idx: (0, idx[12] * 4 + idx[8])),
        ],
        [((ny, q), f32, (r, q), lambda j, idx: (j, 0))], flat_a, b_dec,
    )
    wide_dec = dec_a.astype(f32)
    lengths = jnp.sqrt(jnp.sum(wide_dec * wide_dec, axis=1) + 1e-06)

    (shard,) = local(codes_kernel, [tile], keep, got, b_enc[None, :], active)
    codes = gather(shard, "y", FAR_FIRST)
    codes_other = [exchange(v, "c") for v in codes]

    (recon_own,) = local(
        recon_own_kernel, [sds((rows, half), f32)], *codes, dec, flops=matmul // 2,
        scratch=[pltpu.VMEM((rows, latents), bf16)],
    )

    def recon(blocks, dtypes):
        return local(
            lambda *refs: recon_kernel(blocks, *refs),
            [sds((ny, half), t) for t in dtypes],
            *codes_other, dec_other, recon_own,
            flops=matmul * len(blocks) // 8,
            scratch=[pltpu.VMEM((len(blocks) * ny, latents), bf16)],
        )

    (far,) = recon((2,), (bf16,))
    near_1, near_3, keep = recon((1, 3, 0), (bf16, bf16, f32))
    got = {2: exchange(far, "x", 2), 1: exchange(near_1, "x", 1), 3: exchange(near_3, "x", 3)}
    flat_b, near_3 = after((flat, near_3))
    (acts_t,) = placed(
        turn_acts_kernel, idx, 4,
        [((r, width), lambda j, idx, b=b: (idx[j] * 4 + idx[4 + b], 0)) for b in range(4)],
        [((width, rows), bf16, (width, ny), lambda j, idx: (0, j))], *[flat_b] * 4, size=4 * MIB,
    )
    codes_t, factor = local(
        turn_codes_kernel, [sds((latents, rows), bf16), sds((latents, 1), f32)], *codes, lengths[:, None]
    )
    got[1], acts_t, codes_t = after((got[1], acts_t, codes_t))
    keep, *sends = local(
        split_kernel, [sds((ny, q), f32)] + [sds((ny, q), bf16)] * 3, keep, got[1], got[2], got[3]
    )
    got = {j: exchange(sends[j - 1], "z", j) for j in LINE}
    (error,) = local(error_kernel, [sds((ny, q), bf16)], keep, got[1], got[2], got[3], offset)
    (error,) = local(columns_kernel, [sds((ny, half), bf16)], *gather(error, "z", LINE))
    errors = gather(error, "x", FAR_FIRST)
    errors_other = [exchange(v, "c") for v in errors]

    error_own, back_own = local(
        back_own_kernel, [sds((rows, half), bf16), sds((rows, latents), f32)], *errors, dec, lengths[None, :],
        flops=matmul // 2,
    )
    error_other, *sends, keep = local(
        back_kernel, [sds((rows, half), bf16)] + [tile] * 3 + [sds((ny, latents), f32)],
        *errors_other, dec, back_own,
        flops=matmul // 2,
    )
    keep, got = over_layers(sends, keep)

    m = latents // 4
    grad_dec = pl.pallas_call(
        cross_kernel,
        out_shape=sds((latents, width), bf16),
        grid=(4,),
        in_specs=[
            pl.BlockSpec((m, rows), lambda j: (j, 0)),
            pl.BlockSpec((rows, half), lambda j: (0, 0)),
            pl.BlockSpec((rows, half), lambda j: (0, 0)),
            pl.BlockSpec((m, width), lambda j: (j, 0)),
            pl.BlockSpec((m, 1), lambda j: (j, 0)),
        ],
        out_specs=pl.BlockSpec((m, width), lambda j: (j, 0)),
        compiler_params=LIMIT,
        cost_estimate=cost(matmul, 8 * MIB),
    )(codes_t, error_own, error_other, dec, factor)
    keep, grad_dec = after((keep, grad_dec))
    (shard,) = local(dpre_kernel, [tile], keep, got, active)
    dpre = gather(shard, "y", FAR_FIRST)

    m = width // 8
    grad_enc = pl.pallas_call(
        grad_kernel,
        out_shape=sds((width, latents), bf16),
        grid=(8,),
        in_specs=[pl.BlockSpec(memory_space=pltpu.VMEM)] * 5,
        out_specs=pl.BlockSpec((m, latents), lambda j: (j, 0)),
        scratch_shapes=[pltpu.VMEM((rows, latents), bf16)],
        compiler_params=LIMIT,
        cost_estimate=cost(matmul, 5 * MIB),
    )(acts_t, *dpre)
    return (grad_enc.reshape(w_enc.shape), grad_dec.reshape(w_dec.shape))


def solution(mesh):
    return jax.shard_map(
        body,
        mesh=mesh,
        in_specs=(
            P(None, "layer", None),
            P(None, "latent"),
            P("layer", None, "latent"),
            P("latent"),
            P("latent", "layer", None),
            P("layer", None),
        ),
        out_specs=(P("layer", None, "latent"), P("latent", "layer", None)),
        check_vma=False,
    )
```

```python
import math

import jax
import jax.numpy as jnp
from jax import lax
from jax.experimental import pallas as pl
from jax.experimental.pallas import tpu as pltpu
from jax.sharding import PartitionSpec as P

loss_scale = 0.0625
sparsity = 0.25
bf16 = jnp.bfloat16
f32 = jnp.float32
MIB = 1024 * 1024
FIRST_MIB = 52
LIMIT = pltpu.CompilerParams(vmem_limit_bytes=40 * MIB)
FIRST = pltpu.CompilerParams(vmem_limit_bytes=FIRST_MIB * MIB)
after = lax.optimization_barrier


def place():
    y = lax.axis_index("layer") // 2
    latent = lax.axis_index("latent")
    return y, latent // 2 % 4, latent // 8, latent % 2


def ahead(v, k):
    return (v + k) % 4


def exchange(v, axis, k=1):
    perm = []
    for i in range(256):
        layer, latent = i // 32, i % 32
        y, h = layer // 2, layer % 2
        z, x, c = latent // 8, (latent // 2) % 4, latent % 2
        if axis == "y":
            y = ahead(y, k)
        elif axis == "x":
            x = ahead(x, k)
        elif axis == "z":
            z ^= k
        elif axis == "h":
            h ^= k
        else:
            c ^= k
        perm.append((i, (y * 2 + h) * 32 + (z * 4 + x) * 2 + c))
    return lax.ppermute(v, ("layer", "latent"), perm)


FAR_FIRST = (2, 1, 3)
PARTS = 4
LINE = (3, 2, 1)


def gather(v, axis, ks):
    got = {k: exchange(v, axis, k if axis == "z" else -k) for k in ks}
    return [v, got[1], got[2], got[3]]


def sds(shape, dtype):
    return jax.ShapeDtypeStruct(shape, dtype)


def held(shape, dtype):
    return pltpu.VMEM(shape, dtype)


def cost(flops, size):
    return pl.CostEstimate(flops=flops, bytes_accessed=size, transcendentals=0)


def local(kernel, outs, *args, flops=0, scratch=()):
    in_specs = [
        pl.BlockSpec(memory_space=pltpu.SMEM if a.dtype == jnp.int32 and a.ndim == 1 else pltpu.VMEM) for a in args
    ]
    size = sum(a.size * a.dtype.itemsize for a in args) + sum(math.prod(o.shape) * 4 for o in outs)
    return pl.pallas_call(
        kernel,
        out_shape=outs,
        in_specs=in_specs,
        out_specs=[pl.BlockSpec(memory_space=pltpu.VMEM) for _ in outs],
        scratch_shapes=scratch,
        compiler_params=LIMIT,
        cost_estimate=cost(flops, size),
    )(*args)


def dot(a, b):
    return jnp.dot(a, b, preferred_element_type=f32)


def dot_t(a, b):
    return lax.dot_general(a, b, (((1,), (1,)), ((), ())), preferred_element_type=f32)


def wide(ref):
    return ref[...].astype(f32)


def pre_kernel(acts, enc, *refs):
    sends, keep, total, acts_here, enc_here, sems = refs[:3], *refs[3:]
    m = keep.shape[0]
    k = acts.shape[1] // PARTS
    copies = []
    for i in range(PARTS):
        part = slice(i * k, (i + 1) * k)
        pair = (
            pltpu.make_async_copy(acts.at[:, part], acts_here.at[:, part], sems.at[0, i]),
            pltpu.make_async_copy(enc.at[part, :], enc_here.at[part, :], sems.at[1, i]),
        )
        for copy in pair:
            copy.start()
        copies.append(pair)
    for i, pair in enumerate(copies):
        part = slice(i * k, (i + 1) * k)
        for copy in pair:
            copy.wait()
        value = dot(acts_here[:, part], enc_here[part, :])
        total[...] = value if i == 0 else total[...] + value
    y = place()[0]
    for j, ref in enumerate((keep, *sends)):
        ref[...] = total[pl.ds(pl.multiple_of(ahead(y, j) * m, m), m), :].astype(ref.dtype)


def sum_kernel(keep, a, b, c, out, send):
    total = keep[...] + wide(a) + wide(b) + wide(c)
    out[...] = total
    send[...] = total.astype(bf16)


def codes_kernel(keep, got, bias, active, out):
    r = keep.shape[0] // 4
    for j in range(4):
        rows = pl.ds(pl.multiple_of(ahead(place()[1], j) * r, r), r)
        pre = keep[rows, :] + got[rows, :].astype(f32) + bias[...]
        out[j * r : (j + 1) * r, :] = (active[j * r : (j + 1) * r, :] * pre).astype(bf16)


def recon_own_kernel(*refs):
    own, dec, out, lhs = refs[:4], *refs[4:]
    ny = own[0].shape[0]
    r, half = ny // 4, dec.shape[1] // 2
    for b in range(4):
        for a in range(4):
            lhs[b * ny + a * r : b * ny + (a + 1) * r, :] = own[a][b * r : (b + 1) * r, :]
    c = place()[3]
    out[...] = dot(lhs[...], dec[:, pl.ds(pl.multiple_of(c * half, half), half)])


def recon_kernel(blocks, *refs):
    other, dec, own, outs, lhs = refs[:4], refs[4], refs[5], refs[6:-1], refs[-1]
    ny = other[0].shape[0]
    r = ny // 4
    for i, b in enumerate(blocks):
        for a in range(4):
            lhs[i * ny + a * r : i * ny + (a + 1) * r, :] = other[a][b * r : (b + 1) * r, :]
    value = dot(lhs[...], dec[...])
    for i, (b, out) in enumerate(zip(blocks, outs)):
        out[...] = (value[i * ny : (i + 1) * ny] + own[b * ny : (b + 1) * ny, :]).astype(out.dtype)


def split_kernel(keep, a, b, c, out, *sends):
    q = out.shape[1]
    for j, ref in enumerate((out, *sends)):
        column = pl.ds(pl.multiple_of((place()[2] ^ j) * q, q), q)
        total = keep[:, column] + a[:, column].astype(f32) + b[:, column].astype(f32) + c[:, column].astype(f32)
        ref[...] = total.astype(ref.dtype)


def error_kernel(keep, a, b, c, offset, out):
    out[...] = (keep[...] + wide(a) + wide(b) + wide(c) + offset[...]).astype(bf16)


def columns_kernel(a, b, c, d, out):
    q = a.shape[1]
    for j, ref in enumerate((a, b, c, d)):
        out[:, pl.ds(pl.multiple_of((place()[2] ^ j) * q, q), q)] = ref[...]


def back_own_kernel(*refs):
    own, dec, extra, error, out = refs[:4], *refs[4:]
    rows, half = error.shape
    r, ny = rows // 16, rows // 4
    for a in range(4):
        for b in range(4):
            error[a * ny + b * r : a * ny + (b + 1) * r, :] = own[b][a * r : (a + 1) * r, :]
    c = place()[3]
    out[...] = dot_t(error[...], dec[:, pl.ds(pl.multiple_of(c * half, half), half)]) + sparsity * extra[...]


def back_kernel(*refs):
    other, dec, own, error = refs[:4], *refs[4:7]
    sends, keep = refs[7:10], refs[10]
    rows, half = error.shape
    r, ny = rows // 16, rows // 4
    for a in range(4):
        for b in range(4):
            error[a * ny + b * r : a * ny + (b + 1) * r, :] = other[b][a * r : (a + 1) * r, :]
    c = 1 - place()[3]
    total = own[...] + dot_t(error[...], dec[:, pl.ds(pl.multiple_of(c * half, half), half)])
    for j, ref in enumerate((keep, *sends)):
        ref[...] = total[j * ny : (j + 1) * ny].astype(ref.dtype)


def dpre_kernel(keep, got, active, out):
    out[...] = (loss_scale * active[...] * (keep[...] + wide(got))).astype(bf16)


def copy_kernel(idx, src, out):
    out[...] = src[...].astype(out.dtype)


def offset_kernel(idx, acts, bias, out):
    out[...] = bias[...] - wide(acts)


def turn_acts_kernel(idx, a, b, c, d, out):
    out[...] = jnp.concatenate([a[...], b[...], c[...], d[...]], 0).T


def turn_codes_kernel(a, b, c, d, lengths, out, factor):
    m = a.shape[0]
    for j, ref in enumerate((a, b, c, d)):
        out[:, j * m : (j + 1) * m] = ref[...].T
    usage = jnp.sum(wide(out), axis=1, keepdims=True)
    factor[...] = sparsity * usage / lengths[...]


def cross_kernel(codes, own, other, dec, factor, out):
    half = own.shape[1]
    for c, ref in ((place()[3], own), (1 - place()[3], other)):
        at = pl.ds(pl.multiple_of(c * half, half), half)
        out[:, at] = (loss_scale * (dot(codes[...], ref[...]) + factor[...] * dec[:, at].astype(f32))).astype(bf16)


def grad_kernel(acts, a, b, out):
    m, n = a.shape[0], 512
    rhs = jnp.concatenate([a[...], b[...]], 0)
    for i in range(0, out.shape[0], n):
        out[i : i + n, :] = dot(acts[i : i + n, : 2 * m], rhs)


def grad_rest_kernel(acts, a, b, total, out, rhs):
    m, n = a.shape[0], out.shape[0]
    step = pl.program_id(0)

    @pl.when(step == 0)
    def _():
        rhs[:m, :] = a[...]
        rhs[m:, :] = b[...]

    rows = pl.ds(pl.multiple_of(step * n, n), n)
    out[...] = (total[rows, :] + dot(acts[rows, 2 * m :], rhs[...])).astype(bf16)


def placed(kernel, idx, grid, ins, outs, *args, flops=0, size=MIB, scratch=(), limit=LIMIT):
    return pl.pallas_call(
        kernel,
        out_shape=[sds(o[0], o[1]) for o in outs],
        grid_spec=pltpu.PrefetchScalarGridSpec(
            num_scalar_prefetch=1,
            grid=(grid,),
            in_specs=[pl.BlockSpec(*i) for i in ins],
            out_specs=[pl.BlockSpec(*o[2:]) for o in outs],
            scratch_shapes=scratch,
        ),
        compiler_params=limit,
        cost_estimate=cost(flops, size),
    )(idx, *args)


def body(acts, mask, w_enc, b_enc, w_dec, b_dec):
    rows, _, width = acts.shape
    latents = w_enc.shape[2]
    ny = rows // 4
    r = ny // 4
    half = width // 2
    q = half // 4
    y, x, z, c = place()
    blocks = [ahead(v, k) for v in (y, x) for k in range(4)] + [z ^ k for k in range(4)]
    idx = jnp.stack(blocks + [c, 1 - c]).astype(jnp.int32)
    matmul = 2 * rows * width * latents

    flat = acts.reshape(rows, width)
    enc = w_enc.reshape(width, latents)
    dec = w_dec.reshape(latents, width)
    tile = held((ny, latents), bf16)

    whole = lambda j, idx: (0, 0)
    *sends, keep = pl.pallas_call(
        pre_kernel,
        out_shape=[tile] * 3 + [held((ny, latents), f32)],
        in_specs=[pl.BlockSpec(memory_space=pl.ANY)] * 2,
        out_specs=[pl.BlockSpec(memory_space=pltpu.VMEM)] * 4,
        scratch_shapes=[
            pltpu.VMEM((rows, latents), f32),
            pltpu.VMEM((rows, width), bf16),
            pltpu.VMEM((width, latents), bf16),
            pltpu.SemaphoreType.DMA((2, PARTS)),
        ],
        compiler_params=FIRST,
        cost_estimate=cost(matmul, 6 * MIB),
    )(flat, enc)

    def over_layers(sends, keep):
        got = {j: exchange(sends[j - 1], "y", j) for j in FAR_FIRST}
        keep, send = local(sum_kernel, [held((ny, latents), f32), tile], keep, got[1], got[2], got[3])
        return keep, exchange(send, "h")

    keep, got = over_layers(sends, keep)

    dec_a, mask_a, flat_a, _ = after((dec, mask, flat, keep))
    (dec_send,) = placed(
        copy_kernel, idx, 1, [((latents, half), lambda j, idx: (0, idx[13]))],
        [((latents, half), bf16, (latents, half), whole)], dec_a, size=2 * MIB,
    )
    dec_other = exchange(dec_send, "c")
    (active,) = placed(
        copy_kernel, idx, 4, [((r, latents), lambda j, idx: (idx[0] * 4 + idx[4 + j], 0))],
        [((ny, latents), f32, (r, latents), lambda j, idx: (j, 0))], mask_a,
    )
    (offset,) = placed(
        offset_kernel, idx, 4,
        [
            ((r, q), lambda j, idx: (idx[j] * 4 + idx[4], idx[12] * 4 + idx[8])),
            ((1, q), lambda j, idx: (0, idx[12] * 4 + idx[8])),
        ],
        [((ny, q), f32, (r, q), lambda j, idx: (j, 0))], flat_a, b_dec,
    )
    wide_dec = dec_a.astype(f32)
    lengths = jnp.sqrt(jnp.sum(wide_dec * wide_dec, axis=1) + 1e-06)

    (shard,) = local(codes_kernel, [tile], keep, got, b_enc[None, :], active)
    codes = gather(shard, "y", FAR_FIRST)
    codes_other = [exchange(v, "c") for v in codes]

    (recon_own,) = local(
        recon_own_kernel, [held((rows, half), f32)], *codes, dec, flops=matmul // 2,
        scratch=[pltpu.VMEM((rows, latents), bf16)],
    )

    def recon(blocks, dtypes):
        return local(
            lambda *refs: recon_kernel(blocks, *refs),
            [held((ny, half), t) for t in dtypes],
            *codes_other, dec_other, recon_own,
            flops=matmul * len(blocks) // 8,
            scratch=[pltpu.VMEM((len(blocks) * ny, latents), bf16)],
        )

    (far,) = recon((2,), (bf16,))
    near_1, near_3, keep = recon((1, 3, 0), (bf16, bf16, f32))
    got = {2: exchange(far, "x", 2), 1: exchange(near_1, "x", 1), 3: exchange(near_3, "x", 3)}
    flat_b, near_3 = after((flat, near_3))
    (acts_t,) = placed(
        turn_acts_kernel, idx, 4,
        [((r, width), lambda j, idx, b=b: (idx[j * 3 % 4] * 4 + idx[4 + b], 0)) for b in range(4)],
        [((width, rows), bf16, (width, ny), lambda j, idx: (0, j))], *[flat_b] * 4, size=4 * MIB,
    )
    codes_t, factor = local(
        turn_codes_kernel, [held((latents, rows), bf16), held((latents, 1), f32)], *codes, lengths[:, None]
    )
    got[1], acts_t, codes_t = after((got[1], acts_t, codes_t))
    keep, *sends = local(
        split_kernel, [held((ny, q), f32)] + [held((ny, q), bf16)] * 3, keep, got[1], got[2], got[3]
    )
    got = {j: exchange(sends[j - 1], "z", j) for j in LINE}
    (error,) = local(error_kernel, [held((ny, q), bf16)], keep, got[1], got[2], got[3], offset)
    (error,) = local(columns_kernel, [held((ny, half), bf16)], *gather(error, "z", LINE))
    errors = gather(error, "x", FAR_FIRST)
    errors_other = [exchange(v, "c") for v in errors]

    error_own, back_own = local(
        back_own_kernel, [held((rows, half), bf16), held((rows, latents), f32)], *errors, dec, lengths[None, :],
        flops=matmul // 2,
    )
    error_other, *sends, keep = local(
        back_kernel, [held((rows, half), bf16)] + [tile] * 3 + [held((ny, latents), f32)],
        *errors_other, dec, back_own,
        flops=matmul // 2,
    )
    keep, got = over_layers(sends, keep)

    m = latents // 4
    grad_dec = pl.pallas_call(
        cross_kernel,
        out_shape=sds((latents, width), bf16),
        grid=(4,),
        in_specs=[
            pl.BlockSpec((m, rows), lambda j: (j, 0)),
            pl.BlockSpec((rows, half), lambda j: (0, 0)),
            pl.BlockSpec((rows, half), lambda j: (0, 0)),
            pl.BlockSpec((m, width), lambda j: (j, 0)),
            pl.BlockSpec((m, 1), lambda j: (j, 0)),
        ],
        out_specs=pl.BlockSpec((m, width), lambda j: (j, 0)),
        compiler_params=LIMIT,
        cost_estimate=cost(matmul, 8 * MIB),
    )(codes_t, error_own, error_other, dec, factor)
    keep, grad_dec = after((keep, grad_dec))
    (shard,) = local(dpre_kernel, [tile], keep, got, active)
    dpre = gather(shard, "y", FAR_FIRST)

    (total,) = local(grad_kernel, [held((width, latents), f32)], acts_t, dpre[0], dpre[3], flops=matmul // 2)
    m = width // 4
    grad_enc = pl.pallas_call(
        grad_rest_kernel,
        out_shape=sds((width, latents), bf16),
        grid=(4,),
        in_specs=[pl.BlockSpec(memory_space=pltpu.VMEM)] * 4,
        out_specs=pl.BlockSpec((m, latents), lambda j: (j, 0)),
        scratch_shapes=[pltpu.VMEM((2 * ny, latents), bf16)],
        compiler_params=LIMIT,
        cost_estimate=cost(matmul // 2, 5 * MIB),
    )(acts_t, dpre[2], dpre[1], total)
    return (grad_enc.reshape(w_enc.shape), grad_dec.reshape(w_dec.shape))


def solution(mesh):
    return jax.shard_map(
        body,
        mesh=mesh,
        in_specs=(
            P(None, "layer", None),
            P(None, "latent"),
            P("layer", None, "latent"),
            P("latent"),
            P("latent", "layer", None),
            P("layer", None),
        ),
        out_specs=(P("layer", None, "latent"), P("latent", "layer", None)),
        check_vma=False,
    )
```

```python
import math

import jax
import jax.numpy as jnp
from jax import lax
from jax.experimental import pallas as pl
from jax.experimental.pallas import tpu as pltpu
from jax.sharding import PartitionSpec as P

loss_scale = 0.0625
sparsity = 0.25
bf16 = jnp.bfloat16
f32 = jnp.float32
MIB = 1024 * 1024
FIRST_MIB = 52
LIMIT = pltpu.CompilerParams(vmem_limit_bytes=40 * MIB)
FIRST = pltpu.CompilerParams(vmem_limit_bytes=FIRST_MIB * MIB)
after = lax.optimization_barrier


def place():
    y = lax.axis_index("layer") // 2
    latent = lax.axis_index("latent")
    return y, latent // 2 % 4, latent // 8, latent % 2


def ahead(v, k):
    return (v + k) % 4


def exchange(v, axis, k=1):
    perm = []
    for i in range(256):
        layer, latent = i // 32, i % 32
        y, h = layer // 2, layer % 2
        z, x, c = latent // 8, (latent // 2) % 4, latent % 2
        if axis == "y":
            y = ahead(y, k)
        elif axis == "x":
            x = ahead(x, k)
        elif axis == "z":
            z ^= k
        elif axis == "h":
            h ^= k
        else:
            c ^= k
        perm.append((i, (y * 2 + h) * 32 + (z * 4 + x) * 2 + c))
    return lax.ppermute(v, ("layer", "latent"), perm)


FAR_FIRST = (2, 1, 3)
PARTS = 4
LINE = (1, 2, 3)


def gather(v, axis, ks):
    got = {k: exchange(v, axis, k if axis == "z" else -k) for k in ks}
    return [v, got[1], got[2], got[3]]


def sds(shape, dtype):
    return jax.ShapeDtypeStruct(shape, dtype)


def held(shape, dtype):
    return pltpu.VMEM(shape, dtype)


def cost(flops, size):
    return pl.CostEstimate(flops=flops, bytes_accessed=size, transcendentals=0)


def local(kernel, outs, *args, flops=0, scratch=()):
    in_specs = [
        pl.BlockSpec(memory_space=pltpu.SMEM if a.dtype == jnp.int32 and a.ndim == 1 else pltpu.VMEM) for a in args
    ]
    size = sum(a.size * a.dtype.itemsize for a in args) + sum(math.prod(o.shape) * 4 for o in outs)
    return pl.pallas_call(
        kernel,
        out_shape=outs,
        in_specs=in_specs,
        out_specs=[pl.BlockSpec(memory_space=pltpu.VMEM) for _ in outs],
        scratch_shapes=scratch,
        compiler_params=LIMIT,
        cost_estimate=cost(flops, size),
    )(*args)


def dot(a, b):
    return jnp.dot(a, b, preferred_element_type=f32)


def dot_t(a, b):
    return lax.dot_general(a, b, (((1,), (1,)), ((), ())), preferred_element_type=f32)


def wide(ref):
    return ref[...].astype(f32)


def pre_kernel(acts, enc, *refs):
    sends, keep, total, acts_here, enc_here, sems = refs[:3], *refs[3:]
    m = keep.shape[0]
    k = acts.shape[1] // PARTS
    copies = []
    for i in range(PARTS):
        part = slice(i * k, (i + 1) * k)
        pair = (
            pltpu.make_async_copy(acts.at[:, part], acts_here.at[:, part], sems.at[0, i]),
            pltpu.make_async_copy(enc.at[part, :], enc_here.at[part, :], sems.at[1, i]),
        )
        for copy in pair:
            copy.start()
        copies.append(pair)
    for i, pair in enumerate(copies):
        part = slice(i * k, (i + 1) * k)
        for copy in pair:
            copy.wait()
        value = dot(acts_here[:, part], enc_here[part, :])
        total[...] = value if i == 0 else total[...] + value
    y = place()[0]
    for j, ref in enumerate((keep, *sends)):
        ref[...] = total[pl.ds(pl.multiple_of(ahead(y, j) * m, m), m), :].astype(ref.dtype)


def sum_kernel(keep, a, b, c, out, send):
    total = keep[...] + wide(a) + wide(b) + wide(c)
    out[...] = total
    send[...] = total.astype(bf16)


def codes_kernel(keep, got, bias, active, out):
    r = keep.shape[0] // 4
    for j in range(4):
        rows = pl.ds(pl.multiple_of(ahead(place()[1], j) * r, r), r)
        pre = keep[rows, :] + got[rows, :].astype(f32) + bias[...]
        out[j * r : (j + 1) * r, :] = (active[j * r : (j + 1) * r, :] * pre).astype(bf16)


def recon_own_kernel(*refs):
    own, dec, out, lhs = refs[:4], *refs[4:]
    ny = own[0].shape[0]
    r, half = ny // 4, dec.shape[1] // 2
    for b in range(4):
        for a in range(4):
            lhs[b * ny + a * r : b * ny + (a + 1) * r, :] = own[a][b * r : (b + 1) * r, :]
    c = place()[3]
    out[...] = dot(lhs[...], dec[:, pl.ds(pl.multiple_of(c * half, half), half)])


def recon_kernel(blocks, *refs):
    other, dec, own, outs, lhs = refs[:4], refs[4], refs[5], refs[6:-1], refs[-1]
    ny = other[0].shape[0]
    r = ny // 4
    for i, b in enumerate(blocks):
        for a in range(4):
            lhs[i * ny + a * r : i * ny + (a + 1) * r, :] = other[a][b * r : (b + 1) * r, :]
    value = dot(lhs[...], dec[...])
    for i, (b, out) in enumerate(zip(blocks, outs)):
        out[...] = (value[i * ny : (i + 1) * ny] + own[b * ny : (b + 1) * ny, :]).astype(out.dtype)


def split_kernel(keep, a, b, c, out, *sends):
    q = out.shape[1]
    for j, ref in enumerate((out, *sends)):
        column = pl.ds(pl.multiple_of((place()[2] ^ j) * q, q), q)
        total = keep[:, column] + a[:, column].astype(f32) + b[:, column].astype(f32) + c[:, column].astype(f32)
        ref[...] = total.astype(ref.dtype)


def error_kernel(keep, a, b, c, offset, out):
    out[...] = (keep[...] + wide(a) + wide(b) + wide(c) + offset[...]).astype(bf16)


def columns_kernel(a, b, c, d, out):
    q = a.shape[1]
    for j, ref in enumerate((a, b, c, d)):
        out[:, pl.ds(pl.multiple_of((place()[2] ^ j) * q, q), q)] = ref[...]


def back_own_kernel(*refs):
    own, dec, extra, error, out = refs[:4], *refs[4:]
    rows, half = error.shape
    r, ny = rows // 16, rows // 4
    for a in range(4):
        for b in range(4):
            error[a * ny + b * r : a * ny + (b + 1) * r, :] = own[b][a * r : (a + 1) * r, :]
    c = place()[3]
    out[...] = dot_t(error[...], dec[:, pl.ds(pl.multiple_of(c * half, half), half)]) + sparsity * extra[...]


def back_kernel(*refs):
    other, dec, own, error = refs[:4], *refs[4:7]
    sends, keep = refs[7:10], refs[10]
    rows, half = error.shape
    r, ny = rows // 16, rows // 4
    for a in range(4):
        for b in range(4):
            error[a * ny + b * r : a * ny + (b + 1) * r, :] = other[b][a * r : (a + 1) * r, :]
    c = 1 - place()[3]
    total = own[...] + dot_t(error[...], dec[:, pl.ds(pl.multiple_of(c * half, half), half)])
    for j, ref in enumerate((keep, *sends)):
        ref[...] = total[j * ny : (j + 1) * ny].astype(ref.dtype)


def dpre_kernel(keep, got, active, out):
    out[...] = (loss_scale * active[...] * (keep[...] + wide(got))).astype(bf16)


def copy_kernel(idx, src, out):
    out[...] = src[...].astype(out.dtype)


def offset_kernel(idx, acts, bias, out):
    out[...] = bias[...] - wide(acts)


def turn_acts_kernel(idx, a, b, c, d, out):
    out[...] = jnp.concatenate([a[...], b[...], c[...], d[...]], 0).T


def turn_codes_kernel(a, b, c, d, lengths, out, factor):
    m = a.shape[0]
    for j, ref in enumerate((a, b, c, d)):
        out[:, j * m : (j + 1) * m] = ref[...].T
    usage = jnp.sum(wide(out), axis=1, keepdims=True)
    factor[...] = sparsity * usage / lengths[...]


def cross_kernel(codes, own, other, dec, factor, out):
    half = own.shape[1]
    for c, ref in ((place()[3], own), (1 - place()[3], other)):
        at = pl.ds(pl.multiple_of(c * half, half), half)
        out[:, at] = (loss_scale * (dot(codes[...], ref[...]) + factor[...] * dec[:, at].astype(f32))).astype(bf16)


def grad_kernel(acts, a, b, out):
    m, n = a.shape[0], 512
    rhs = jnp.concatenate([a[...], b[...]], 0)
    for i in range(0, out.shape[0], n):
        out[i : i + n, :] = dot(acts[i : i + n, : 2 * m], rhs)


def grad_rest_kernel(acts, a, b, total, out, rhs):
    m, n = a.shape[0], out.shape[0]
    step = pl.program_id(0)

    @pl.when(step == 0)
    def _():
        rhs[:m, :] = a[...]
        rhs[m:, :] = b[...]

    rows = pl.ds(pl.multiple_of(step * n, n), n)
    out[...] = (total[rows, :] + dot(acts[rows, 2 * m :], rhs[...])).astype(bf16)


def placed(kernel, idx, grid, ins, outs, *args, flops=0, size=MIB, scratch=(), limit=LIMIT):
    return pl.pallas_call(
        kernel,
        out_shape=[sds(o[0], o[1]) for o in outs],
        grid_spec=pltpu.PrefetchScalarGridSpec(
            num_scalar_prefetch=1,
            grid=(grid,),
            in_specs=[pl.BlockSpec(*i) for i in ins],
            out_specs=[pl.BlockSpec(*o[2:]) for o in outs],
            scratch_shapes=scratch,
        ),
        compiler_params=limit,
        cost_estimate=cost(flops, size),
    )(idx, *args)


def body(acts, mask, w_enc, b_enc, w_dec, b_dec):
    rows, _, width = acts.shape
    latents = w_enc.shape[2]
    ny = rows // 4
    r = ny // 4
    half = width // 2
    q = half // 4
    y, x, z, c = place()
    blocks = [ahead(v, k) for v in (y, x) for k in range(4)] + [z ^ k for k in range(4)]
    idx = jnp.stack(blocks + [c, 1 - c]).astype(jnp.int32)
    matmul = 2 * rows * width * latents

    flat = acts.reshape(rows, width)
    enc = w_enc.reshape(width, latents)
    dec = w_dec.reshape(latents, width)
    tile = held((ny, latents), bf16)

    whole = lambda j, idx: (0, 0)
    *sends, keep = pl.pallas_call(
        pre_kernel,
        out_shape=[tile] * 3 + [held((ny, latents), f32)],
        in_specs=[pl.BlockSpec(memory_space=pl.ANY)] * 2,
        out_specs=[pl.BlockSpec(memory_space=pltpu.VMEM)] * 4,
        scratch_shapes=[
            pltpu.VMEM((rows, latents), f32),
            pltpu.VMEM((rows, width), bf16),
            pltpu.VMEM((width, latents), bf16),
            pltpu.SemaphoreType.DMA((2, PARTS)),
        ],
        compiler_params=FIRST,
        cost_estimate=cost(matmul, 6 * MIB),
    )(flat, enc)

    def over_layers(sends, keep):
        got = {j: exchange(sends[j - 1], "y", j) for j in FAR_FIRST}
        keep, send = local(sum_kernel, [held((ny, latents), f32), tile], keep, got[1], got[2], got[3])
        return keep, exchange(send, "h")

    keep, got = over_layers(sends, keep)

    dec_a, mask_a, flat_a, _ = after((dec, mask, flat, keep))
    (dec_send,) = placed(
        copy_kernel, idx, 1, [((latents, half), lambda j, idx: (0, idx[13]))],
        [((latents, half), bf16, (latents, half), whole)], dec_a, size=2 * MIB,
    )
    dec_other = exchange(dec_send, "c")
    (active,) = placed(
        copy_kernel, idx, 4, [((r, latents), lambda j, idx: (idx[0] * 4 + idx[4 + j], 0))],
        [((ny, latents), f32, (r, latents), lambda j, idx: (j, 0))], mask_a,
    )
    (offset,) = placed(
        offset_kernel, idx, 4,
        [
            ((r, q), lambda j, idx: (idx[j] * 4 + idx[4], idx[12] * 4 + idx[8])),
            ((1, q), lambda j, idx: (0, idx[12] * 4 + idx[8])),
        ],
        [((ny, q), f32, (r, q), lambda j, idx: (j, 0))], flat_a, b_dec,
    )
    wide_dec = dec_a.astype(f32)
    lengths = jnp.sqrt(jnp.sum(wide_dec * wide_dec, axis=1) + 1e-06)

    (shard,) = local(codes_kernel, [tile], keep, got, b_enc[None, :], active)
    codes = gather(shard, "y", FAR_FIRST)
    codes_other = [exchange(v, "c") for v in codes]

    (recon_own,) = local(
        recon_own_kernel, [held((rows, half), f32)], *codes, dec, flops=matmul // 2,
        scratch=[pltpu.VMEM((rows, latents), bf16)],
    )

    def recon(blocks, dtypes):
        return local(
            lambda *refs: recon_kernel(blocks, *refs),
            [held((ny, half), t) for t in dtypes],
            *codes_other, dec_other, recon_own,
            flops=matmul * len(blocks) // 8,
            scratch=[pltpu.VMEM((len(blocks) * ny, latents), bf16)],
        )

    (far,) = recon((2,), (bf16,))
    near_1, near_3, keep = recon((1, 3, 0), (bf16, bf16, f32))
    got = {2: exchange(far, "x", 2), 1: exchange(near_1, "x", 1), 3: exchange(near_3, "x", 3)}
    flat_b, near_3 = after((flat, near_3))
    (acts_t,) = placed(
        turn_acts_kernel, idx, 4,
        [((r, width), lambda j, idx, b=b: (idx[j * 3 % 4] * 4 + idx[4 + b], 0)) for b in range(4)],
        [((width, rows), bf16, (width, ny), lambda j, idx: (0, j))], *[flat_b] * 4, size=4 * MIB,
    )
    codes_t, factor = local(
        turn_codes_kernel, [held((latents, rows), bf16), held((latents, 1), f32)], *codes, lengths[:, None]
    )
    got[1], acts_t, codes_t = after((got[1], acts_t, codes_t))
    keep, *sends = local(
        split_kernel, [held((ny, q), f32)] + [held((ny, q), bf16)] * 3, keep, got[1], got[2], got[3]
    )
    got = {j: exchange(sends[j - 1], "z", j) for j in LINE}
    (error,) = local(error_kernel, [held((ny, q), bf16)], keep, got[1], got[2], got[3], offset)
    (error,) = local(columns_kernel, [held((ny, half), bf16)], *gather(error, "z", LINE))
    errors = gather(error, "x", FAR_FIRST)
    errors_other = [exchange(v, "c") for v in errors]

    error_own, back_own = local(
        back_own_kernel, [held((rows, half), bf16), held((rows, latents), f32)], *errors, dec, lengths[None, :],
        flops=matmul // 2,
    )
    error_other, *sends, keep = local(
        back_kernel, [held((rows, half), bf16)] + [tile] * 3 + [held((ny, latents), f32)],
        *errors_other, dec, back_own,
        flops=matmul // 2,
    )
    keep, got = over_layers(sends, keep)

    m = latents // 4
    grad_dec = pl.pallas_call(
        cross_kernel,
        out_shape=sds((latents, width), bf16),
        grid=(4,),
        in_specs=[
            pl.BlockSpec((m, rows), lambda j: (j, 0)),
            pl.BlockSpec((rows, half), lambda j: (0, 0)),
            pl.BlockSpec((rows, half), lambda j: (0, 0)),
            pl.BlockSpec((m, width), lambda j: (j, 0)),
            pl.BlockSpec((m, 1), lambda j: (j, 0)),
        ],
        out_specs=pl.BlockSpec((m, width), lambda j: (j, 0)),
        compiler_params=LIMIT,
        cost_estimate=cost(matmul, 8 * MIB),
    )(codes_t, error_own, error_other, dec, factor)
    keep, grad_dec = after((keep, grad_dec))
    (shard,) = local(dpre_kernel, [tile], keep, got, active)
    dpre = gather(shard, "y", FAR_FIRST)

    (total,) = local(grad_kernel, [held((width, latents), f32)], acts_t, dpre[0], dpre[3], flops=matmul // 2)
    m = width // 4
    grad_enc = pl.pallas_call(
        grad_rest_kernel,
        out_shape=sds((width, latents), bf16),
        grid=(4,),
        in_specs=[pl.BlockSpec(memory_space=pltpu.VMEM)] * 4,
        out_specs=pl.BlockSpec((m, latents), lambda j: (j, 0)),
        scratch_shapes=[pltpu.VMEM((2 * ny, latents), bf16)],
        compiler_params=LIMIT,
        cost_estimate=cost(matmul // 2, 5 * MIB),
    )(acts_t, dpre[2], dpre[1], total)
    return (grad_enc.reshape(w_enc.shape), grad_dec.reshape(w_dec.shape))


def solution(mesh):
    return jax.shard_map(
        body,
        mesh=mesh,
        in_specs=(
            P(None, "layer", None),
            P(None, "latent"),
            P("layer", None, "latent"),
            P("latent"),
            P("latent", "layer", None),
            P("layer", None),
        ),
        out_specs=(P("layer", None, "latent"), P("latent", "layer", None)),
        check_vma=False,
    )
```
